32 devices in a mesh: dp: 32 (over z, y, x, core).
Axes of the slice: x: 2, y: 2, z: 4, core: 2. Of those that a mesh axis runs over, the one named last changes fastest.
Arguments:
- hidden_in: bfloat16 [8192, 1024], P('dp'), may hold values from -6 to 6
- segments: int32 [8192], replicated, may hold values from 0 to 47, as said below
- routes: int32 [8192, 8], P('dp'), may hold values from 0 to 31, all different within a row; in each aligned block of 256 rows (0 to 255, 256 to 511, ...) at most 80 rows name the same one
- attn_gain: float32 [1024], replicated, may hold values from 0.5 to 1.5
- w_query: bfloat16 [1024, 1024], replicated, may hold values from -0.1875 to 0.1875
- w_key: bfloat16 [1024, 512], replicated, may hold values from -0.1875 to 0.1875
- w_value: bfloat16 [1024, 512], replicated, may hold values from -0.1875 to 0.1875
- w_out: bfloat16 [1024, 1024], replicated, may hold values from -0.75 to 0.75
- moe_gain: float32 [1024], replicated, may hold values from 0.5 to 1.5
- w_router: bfloat16 [1024, 32], replicated, may hold values from -0.09375 to 0.09375
- w_gate: bfloat16 [1024, 16384], P(None, 'dp'), may hold values from -0.1875 to 0.1875
- w_up: bfloat16 [1024, 16384], P(None, 'dp'), may hold values from -0.1875 to 0.1875
- w_down: bfloat16 [16384, 1024], P('dp'), may hold values from -1 to 1
- d_out: bfloat16 [8192, 1024], P('dp'), may hold values from -6 to 6
Outputs:
- out_hidden: bfloat16 [8192, 1024], P('dp')
- grad_input: float32 [8192, 1024], P('dp')
- grad_attn_gain: float32 [1024], P('dp')
- grad_query: float32 [1024, 1024], P('dp')
- grad_key: float32 [1024, 512], P('dp')
- grad_value: float32 [1024, 512], P('dp')
- grad_out: float32 [1024, 1024], P(None, 'dp')
- grad_moe_gain: float32 [1024], P('dp')
- grad_router: float32 [1024, 32], P('dp')
- grad_gate: float32 [1024, 16384], P(None, 'dp')
- grad_up: float32 [1024, 16384], P(None, 'dp')
- grad_down: float32 [16384, 1024], P('dp')
The draws below stay inside these ranges and needn't reach their ends.
Inputs may be any that keep to these rules, and one draw needn't show every extreme that they name: `segments`: segment numbers never fall along the tokens, and tokens of different sequences of 512 tokens have different numbers. `routes`: among the rows of one device no expert is named by more than 80 rows.
All inputs are finite; a program needn't handle non-finite values.
Results may differ from the reference program's by a relative error of at most 0.017.
Values may be sent and summed in bfloat16 or wider, within the bound.
A program may use at most 256 MiB of HBM per device.

```python
import math
import jax
import jax.numpy as jnp
import numpy as np
from jax import lax

D = 1024
HEADS = 16
KV_HEADS = 8
HEAD_DIM = 64
EXPERTS = 32
FF = 512
TOP = 8
TOK_DEV = 256
SEQ_LEN = 512
TOKENS = 8192
CAP = 80
N_DP = 32


def draw_segments(key, part):
    key = jax.random.fold_in(key, 11)
    first_key, second_key = jax.random.split(key)
    seq_total = TOKENS // SEQ_LEN
    first_cut = jax.random.randint(first_key, (seq_total,), 1, SEQ_LEN // 4)
    second_cut = jax.random.randint(second_key, (seq_total,), 3 * SEQ_LEN // 4 + 1, SEQ_LEN)
    places = jnp.arange(SEQ_LEN, dtype=jnp.int32)[None, :]
    inside = (places >= first_cut[:, None]).astype(jnp.int32) + (places >= second_cut[:, None]).astype(jnp.int32)
    numbers = inside + 3 * jnp.arange(seq_total, dtype=jnp.int32)[:, None]
    return numbers.reshape(-1).astype(jnp.int32)


def level_of(rng, shape, cuts, smallest, high):
    factor_of = 1.0
    for dim, parts in cuts:
        draws = jax.random.uniform(jax.random.fold_in(jax.random.fold_in(rng, 6), dim), (parts,), jnp.float32, smallest / len(cuts), high / len(cuts))
        factor_of = factor_of * jnp.repeat(jnp.exp(draws), shape[dim] // parts).reshape((-1,) + (1,) * (len(shape) - 1 - dim))
    return factor_of


def deal_out(own_key, own, number, rows, amount, top, most, lean):
    ranking = jax.random.permutation(own_key, amount)
    crowded, common = portions_of(amount, rows * top, most, lean, True), portions_of(amount, rows * top, most, lean, False)
    places = jnp.arange(amount)

    def named(sizes, turn):
        used = int((sizes > 0).sum())
        fixed = max(1, used // 4)
        moved = fixed + (places - fixed + turn * (used - fixed)) % max(1, amount - fixed)
        return jnp.zeros((amount,), jnp.int32).at[ranking[jnp.where(places < fixed, places, moved)]].set(jnp.asarray(sizes, jnp.int32))

    sizes = jnp.where(number % 4 == 0, named(crowded, number // 4), named(common, number - number // 4 - 1))
    mixed = jax.random.permutation(jax.random.fold_in(own, 3), amount)
    donor, sink = mixed[0:amount // 2 * 2:2], mixed[1:amount // 2 * 2:2]
    slack = jnp.minimum(sizes[donor] - 1, most - sizes[sink]) // 2
    slack = jnp.where((donor == ranking[0]) | (sink == ranking[0]) | (sizes[sink] == 0), 0, jnp.maximum(slack, 0))
    moved = jax.random.randint(jax.random.fold_in(own, 4), (amount // 2,), 0, 1 << 20) % (slack + 1)
    sizes = sizes.at[donor].add(-moved).at[sink].add(moved)
    labels = jnp.searchsorted(jnp.cumsum(sizes), jnp.arange(rows * top), side="right").astype(jnp.int32)
    listing = labels.reshape(top, rows).T
    listing = listing[jax.random.permutation(jax.random.fold_in(own, 1), rows)]
    turn = jax.random.randint(jax.random.fold_in(own, 2), (rows, 1), 0, top)
    return jnp.take_along_axis(listing, (jnp.arange(top)[None, :] + turn) % top, axis=1)


def portions_of(count, total, limit, skew, full):
    portions = [(1 << 20) // math.isqrt(rank ** skew) + 1 for rank in range(1, count + 1)]
    largest = limit if full else min(limit, max(-(-total // count), total * portions[0] // sum(portions)))
    least = 1 if total - largest >= count - 1 else 0
    given, surplus = [largest] + [least] * (count - 1), total - largest - least * (count - 1)
    while surplus > 0:
        movable = [i for i in range(1, count) if given[i] < largest] or [i for i in range(1, count) if given[i] < limit]
        mass, remaining = sum([portions[i] for i in movable]), surplus
        for i in movable:
            more = min(limit - given[i], max(1, remaining * portions[i] // mass), surplus)
            given[i] = given[i] + more
            surplus = surplus - more
    return np.array(given)


def scatter_about(rng, dims, deviation, bound, shards=(), kind=jnp.bfloat16):
    drawn = jax.random.normal(rng, dims, jnp.float32) * deviation
    if len(shards) > 0:
        drawn = level_of(rng, dims, shards, -0.22, 0.18) * drawn
    return jnp.clip(drawn, min=-bound, max=bound).astype(kind)


def setup_inputs(seed: int = 0) -> dict:
    arg_keys = jax.random.split(jax.random.key(seed), 15)
    hidden_in = scatter_about(arg_keys[0], (TOKENS, D), 1.0, 6.0, ((0, 32),))
    segments = draw_segments(jax.random.fold_in(arg_keys[14], 71), 0)
    routes_keys = jax.random.split(jax.random.fold_in(arg_keys[2], 1), TOKENS // TOK_DEV)
    routes_turns = jax.random.permutation(jax.random.fold_in(arg_keys[2], 3), TOKENS // TOK_DEV)
    routes = jax.vmap(lambda own, number: deal_out(jax.random.fold_in(arg_keys[2], 2), own, number, TOK_DEV, EXPERTS, TOP, CAP, 0))(routes_keys, routes_turns).reshape((TOKENS, TOP))
    attn_gain = jnp.clip(1.0 + 0.1 * jax.random.normal(arg_keys[3], (D,), jnp.float32), 0.5, 1.5)
    w_query = scatter_about(arg_keys[4], (D, HEADS * HEAD_DIM), D ** -0.5, 0.1875)
    w_key = scatter_about(arg_keys[5], (D, KV_HEADS * HEAD_DIM), D ** -0.5, 0.1875)
    w_value = scatter_about(arg_keys[6], (D, KV_HEADS * HEAD_DIM), D ** -0.5, 0.1875)
    w_out = scatter_about(arg_keys[7], (HEADS * HEAD_DIM, D), (HEADS * HEAD_DIM // 16) ** -0.5, 0.75)
    moe_gain = jnp.clip(1.0 + 0.1 * jax.random.normal(arg_keys[8], (D,), jnp.float32), 0.5, 1.5)
    w_router = scatter_about(arg_keys[9], (D, EXPERTS), 0.015625, 0.09375)
    w_gate = scatter_about(arg_keys[10], (D, EXPERTS * FF), D ** -0.5, 0.1875, ((1, 32),))
    w_up = scatter_about(arg_keys[11], (D, EXPERTS * FF), D ** -0.5, 0.1875, ((1, 32),))
    w_down = scatter_about(arg_keys[12], (EXPERTS * FF, D), (FF // 16) ** -0.5, 1.0, ((0, 32),))
    d_out = scatter_about(arg_keys[13], (TOKENS, D), 1.0, 6.0, ((0, 32),))
    return {"hidden_in": hidden_in, "segments": segments, "routes": routes, "attn_gain": attn_gain, "w_query": w_query, "w_key": w_key, "w_value": w_value, "w_out": w_out, "moe_gain": moe_gain, "w_router": w_router, "w_gate": w_gate, "w_up": w_up, "w_down": w_down, "d_out": d_out}


EPSILON = 1e-06
HIGHEST = lax.Precision.HIGHEST

@jax.custom_vjp
def low(v):
    return lax.optimization_barrier(v.astype(jnp.bfloat16)).astype(jnp.float32)

@jax.custom_vjp
def low_back(v):
    return v

def low_keep(v):
    return (low(v), None)

def low_pass(kept, grad):
    return (grad,)

def back_keep(v):
    return (v, None)

def back_low(kept, grad):
    return (low(grad),)
low.defvjp(low_keep, low_pass)
low_back.defvjp(back_keep, back_low)

def rms_scale(values, gain):
    return values * lax.rsqrt(lax.optimization_barrier(jnp.mean(values * values, axis=-1, keepdims=True)) + EPSILON) * gain

def rope_tables(positions, head_size):
    half_size = head_size // 2
    freqs = jnp.power(10000.0, -jnp.arange(half_size, dtype=jnp.float32) / half_size)
    angles = positions.astype(jnp.float32)[:, None] * freqs[None, :]
    angles = jnp.concatenate([angles, angles], axis=1)
    return (jnp.cos(angles), jnp.sin(angles))

def rotate(values, cosine, sine):
    half_size = values.shape[-1] // 2
    turned = jnp.concatenate([-values[..., half_size:], values[..., :half_size]], axis=-1)
    return values * cosine[:, None, :] + turned * sine[:, None, :]

def slot_table(route_rows):
    flat_routes = route_rows.reshape(-1)
    onehot = (flat_routes[:, None] == jnp.arange(EXPERTS, dtype=jnp.int32)[None, :]).astype(jnp.int32)
    ranks = lax.optimization_barrier(jnp.sum((jnp.cumsum(onehot, axis=0) - onehot) * onehot, axis=1))
    slots = flat_routes * CAP + ranks
    owners = jnp.arange(flat_routes.shape[0], dtype=jnp.int32) // route_rows.shape[1]
    token_of = jnp.zeros((EXPERTS * CAP,), jnp.int32).at[slots].set(owners)
    filled = jnp.zeros((EXPERTS * CAP,), jnp.float32).at[slots].set(1.0)
    return (slots, token_of, filled)

def layer(x_float, attn_gain, w_query, w_key, w_value, w_out, moe_gain, w_router, w_gate, w_up, w_down, seg_rows, route_rows):
    length = x_float.shape[0]
    groups = HEADS // KV_HEADS
    score_scale = 1.0 / math.sqrt(HEAD_DIM)
    h_one = low(rms_scale(x_float, attn_gain))
    cosine, sine = rope_tables(jnp.arange(length, dtype=jnp.int32), HEAD_DIM)
    q_raw = low_back(jnp.dot(h_one, w_query, precision=HIGHEST)).reshape(length, HEADS, HEAD_DIM)
    k_raw = low_back(jnp.dot(h_one, w_key, precision=HIGHEST)).reshape(length, KV_HEADS, HEAD_DIM)
    v_low = low(low_back(jnp.dot(h_one, w_value, precision=HIGHEST))).reshape(length, KV_HEADS, HEAD_DIM)
    q_rot = low(rotate(q_raw, cosine, sine))
    k_rot = low(rotate(k_raw, cosine, sine))
    places = jnp.arange(length, dtype=jnp.int32)
    allowed = (seg_rows[:, None] == seg_rows[None, :]) & (places[None, :] <= places[:, None])
    block_rows = min(512, length)
    num_blocks = length // block_rows
    q_blocks = q_rot.reshape(num_blocks, block_rows, KV_HEADS, groups, HEAD_DIM)
    a_blocks = allowed.reshape(num_blocks, block_rows, length)

    def attend(pieces):
        queries, allow = pieces
        raw = jnp.einsum('qcgd,kcd->cgqk', queries, k_rot, precision=HIGHEST)
        scores = low_back(jnp.where(allow[None, None], raw * score_scale, -1e+30))
        probs = jax.nn.softmax(scores, axis=-1)
        return jnp.einsum('cgqk,kcd->qcgd', low(probs), v_low, precision=HIGHEST)
    attended = lax.map(jax.checkpoint(attend), (q_blocks, a_blocks))
    o_low = low(low_back(attended.reshape(length, HEADS * HEAD_DIM)))
    r_one = x_float + low_back(jnp.dot(o_low, w_out, precision=HIGHEST))
    h_two = low(rms_scale(r_one, moe_gain))
    logits = low_back(jnp.dot(h_two, w_router, precision=HIGHEST))
    gates = jax.nn.softmax(jnp.take_along_axis(logits, route_rows, axis=1), axis=-1)
    dev_blocks = length // TOK_DEV
    slots, token_of, filled = jax.vmap(slot_table)(route_rows.reshape(dev_blocks, TOK_DEV, TOP))
    block_ids = jnp.arange(dev_blocks, dtype=jnp.int32)[:, None]
    all_slots = (slots + block_ids * (EXPERTS * CAP)).reshape(-1)
    all_tokens = (token_of + block_ids * TOK_DEV).reshape(-1)
    all_filled = filled.reshape(-1)
    arrived = h_two[all_tokens] * all_filled[:, None]
    arrived = arrived.reshape(dev_blocks, EXPERTS, CAP, D).transpose(1, 0, 2, 3).reshape(EXPERTS, dev_blocks * CAP, D)
    split_ways = N_DP // EXPERTS
    part_width = FF // split_ways
    gate_w = w_gate.reshape(D, EXPERTS, split_ways, part_width).transpose(1, 2, 0, 3)
    up_w = w_up.reshape(D, EXPERTS, split_ways, part_width).transpose(1, 2, 0, 3)
    down_w = w_down.reshape(EXPERTS, split_ways, part_width, D)
    expert_out = jnp.zeros((EXPERTS, dev_blocks * CAP, D), jnp.float32)
    for part_index in range(split_ways):
        part_rows = low_back(arrived)
        gate_pre = low_back(jnp.einsum('erd,edf->erf', part_rows, gate_w[:, part_index], precision=HIGHEST))
        up_pre = low_back(jnp.einsum('erd,edf->erf', part_rows, up_w[:, part_index], precision=HIGHEST))
        hidden = low(jax.nn.silu(gate_pre) * up_pre)
        partial_out = jnp.einsum('erf,efd->erd', hidden, down_w[:, part_index], precision=HIGHEST)
        expert_out = expert_out + low(low_back(partial_out))
    expert_out = expert_out.reshape(EXPERTS, dev_blocks, CAP, D).transpose(1, 0, 2, 3).reshape(-1, D)
    per_route = expert_out[all_slots].reshape(length, TOP, D)
    mixed = lax.optimization_barrier(jnp.sum(gates[:, :, None] * per_route, axis=1))
    return r_one + mixed

def reference(hidden_in, segments, routes, attn_gain, w_query, w_key, w_value, w_out, moe_gain, w_router, w_gate, w_up, w_down, d_out):
    weights = tuple((w.astype(jnp.float32) for w in (attn_gain, w_query, w_key, w_value, w_out, moe_gain, w_router, w_gate, w_up, w_down)))
    seq_total = hidden_in.shape[0] // SEQ_LEN
    pieces = (hidden_in.reshape(seq_total, SEQ_LEN, D), d_out.reshape(seq_total, SEQ_LEN, D), routes.reshape(seq_total, SEQ_LEN, TOP), segments.reshape(seq_total, SEQ_LEN))

    def one_sequence(totals, items):
        x_rows, cot_rows, route_rows, seg_rows = items
        x_float = x_rows.astype(jnp.float32)

        def forward(x_value, *params):
            return layer(x_value, *params, seg_rows, route_rows)
        result, pullback = jax.vjp(forward, x_float, *weights)
        grads = pullback(cot_rows.astype(jnp.float32))
        totals = tuple((a + b for a, b in zip(totals, grads[1:])))
        return (totals, (result.astype(jnp.bfloat16), grads[0]))
    start = tuple((jnp.zeros_like(w) for w in weights))
    totals, (results, input_grads) = lax.scan(one_sequence, start, pieces)
    return (results.reshape(-1, D), input_grads.reshape(-1, D), totals[0], totals[1], totals[2], totals[3], totals[4], totals[5], totals[6], totals[7], totals[8], totals[9])
```

```python
import math

import jax
import jax.numpy as jnp
from jax import lax
from jax.sharding import PartitionSpec as P

HEADS = 16
KV_HEADS = 8
HEAD_DIM = 64
TOP = 8
CAP = 80


EPSILON = 1e-06


def passed_along(value, axis, steps):
    count = lax.axis_size(axis)
    leading, last = (max(0, -steps), min(count, count - steps))
    return lax.ppermute(value, axis, [(source, source + steps) for source in range(leading, last)])


def rms_scale(values, gain):
    return values * lax.rsqrt(jnp.mean(values * values, axis=-1, keepdims=True) + EPSILON) * gain


def rope_tables(positions, head_size):
    half_size = head_size // 2
    freqs = jnp.power(10000.0, -jnp.arange(half_size, dtype=jnp.float32) / half_size)
    angles = positions.astype(jnp.float32)[:, None] * freqs[None, :]
    angles = jnp.concatenate([angles, angles], axis=1)
    return (jnp.cos(angles), jnp.sin(angles))


def rotate(values, cosine, sine):
    half_size = values.shape[-1] // 2
    turned = jnp.concatenate([-values[..., half_size:], values[..., :half_size]], axis=-1)
    return values * cosine[:, None, :] + turned * sine[:, None, :]


def unrotate(grads, cosine, sine):
    half_size = grads.shape[-1] // 2
    moved = grads * sine[:, None, :]
    return grads * cosine[:, None, :] + jnp.concatenate(
        [moved[..., half_size:], -moved[..., :half_size]], axis=-1
    )


def dot_right_t(left, right):
    return lax.dot_general(
        left, right, (((1,), (1,)), ((), ())), preferred_element_type=jnp.float32
    )


def dot_left_t(left, right):
    return lax.dot_general(
        left, right, (((0,), (0,)), ((), ())), preferred_element_type=jnp.float32
    )


def split_two(values):
    high = values.astype(jnp.bfloat16)
    rest = (values - high.astype(jnp.float32)).astype(jnp.bfloat16)
    return high, rest


def member_mask(route_rows, num_experts):
    ids = jnp.arange(num_experts, dtype=jnp.int32)
    return jnp.any(route_rows[:, :, None] == ids[None, None, :], axis=1)


def placement(mask, first, amount):
    tok_count = mask.shape[0]
    part = lax.dynamic_slice_in_dim(mask.astype(jnp.bfloat16), first, amount, axis=1)
    places = jnp.arange(tok_count, dtype=jnp.int32)
    earlier = (places[:, None] < places[None, :]).astype(jnp.bfloat16)
    ranks = dot_left_t(part, earlier)
    ranks = jnp.where(part.T > 0, ranks, -1.0)
    want = jnp.arange(CAP, dtype=jnp.int32).astype(jnp.float32)
    chosen = (ranks[:, None, :] == want[None, :, None]).astype(jnp.bfloat16)
    return chosen.reshape(amount * CAP, tok_count)


def spread(chosen, values, amount, split_ways, groups):
    width = values.shape[1]
    picked = jnp.dot(chosen, values, preferred_element_type=jnp.float32).astype(jnp.bfloat16)
    sent = jnp.broadcast_to(
        picked.reshape(amount, 1, CAP, width), (amount, split_ways, CAP, width)
    ).reshape(amount * split_ways, CAP, width)
    return lax.all_to_all(
        sent, "dp", split_axis=0, concat_axis=0, tiled=True, axis_index_groups=groups
    ).reshape(-1, width)


def bring_back(chosen, rows, amount, split_ways, groups):
    width = rows.shape[1]
    back = lax.all_to_all(
        rows.reshape(amount * split_ways, CAP, width),
        "dp",
        split_axis=0,
        concat_axis=0,
        tiled=True,
        axis_index_groups=groups,
    ).reshape(-1, width)
    if split_ways > 1:
        tok_count = chosen.shape[1]
        chosen = jnp.broadcast_to(
            chosen.reshape(amount, 1, CAP, tok_count), (amount, split_ways, CAP, tok_count)
        ).reshape(-1, tok_count)
    return back, chosen


def expert_block(rows, gate, cot_rows, w_gate, w_up, w_down):
    gate_pre = jnp.dot(rows, w_gate, preferred_element_type=jnp.float32)
    up_pre = jnp.dot(rows, w_up, preferred_element_type=jnp.float32)
    sigmoid = jax.nn.sigmoid(gate_pre)
    activated = gate_pre * sigmoid
    hidden = (activated * up_pre).astype(jnp.bfloat16)
    cot_float = cot_rows.astype(jnp.float32)
    grad_rows = (gate * cot_float).astype(jnp.bfloat16)
    grad_hidden = dot_right_t(grad_rows, w_down)
    grad_gate_pre = (grad_hidden * up_pre * (sigmoid * (1.0 + gate_pre * (1.0 - sigmoid)))).astype(
        jnp.bfloat16
    )
    grad_up_pre = (grad_hidden * activated).astype(jnp.bfloat16)
    back = (dot_right_t(grad_gate_pre, w_gate) + dot_right_t(grad_up_pre, w_up)).astype(
        jnp.bfloat16
    )
    expert_out = jnp.dot(hidden, w_down, preferred_element_type=jnp.float32)
    grad_gates = jnp.sum(expert_out * cot_float, axis=1, keepdims=True)
    gated_out = (gate * expert_out).astype(jnp.bfloat16)
    return (hidden, grad_rows, grad_gate_pre, grad_up_pre, back, grad_gates, gated_out)


def reduced(parts, extras, devices):
    sizes = (2, 4, devices // 8)
    rows = parts.shape[0] // devices
    width = parts.shape[1]
    extra_width = extras.shape[1]
    filler = jnp.zeros((parts.shape[0], 128 - 2 * extra_width), jnp.bfloat16)
    grid = (sizes[2], sizes[1], sizes[0], rows, -1)
    main, extra = parts.reshape(grid), extras.reshape(grid)
    filler = filler.reshape(grid)
    stage_groups = (
        [[2 * i, 2 * i + 1] for i in range(devices // 2)],
        [[8 * z + 2 * i + c for i in range(4)] for z in range(devices // 8) for c in range(2)],
        [[8 * z + i for z in range(devices // 8)] for i in range(8)],
    )
    for groups, size in zip(stage_groups, sizes):
        high, rest = split_two(extra)
        packed = jnp.concatenate([main.astype(jnp.bfloat16), high, rest, filler], axis=-1)
        axis = packed.ndim - 3
        packed = jnp.moveaxis(packed, axis, 0)
        got = lax.all_to_all(
            packed, "dp", split_axis=0, concat_axis=0, tiled=True, axis_index_groups=groups
        )
        total = jnp.sum(got.astype(jnp.float32), axis=0)
        main = total[..., :width]
        extra = (
            total[..., width : width + extra_width]
            + total[..., width + extra_width : width + 2 * extra_width]
        )
        filler = filler.reshape((-1,) + filler.shape[-2:])[: math.prod(total.shape[:-2])]
        filler = filler.reshape(total.shape[:-1] + (filler.shape[-1],))
    return main, extra


def block_scores(queries, key_rows, allow, score_scale):
    raw = jnp.einsum("qcgd,kcd->cgqk", queries, key_rows, preferred_element_type=jnp.float32)
    return jnp.where(allow[None, None], raw * score_scale, -1e30)


def forward_block(queries, key_rows, value_rows, allow, score_scale):
    scores = block_scores(queries, key_rows, allow, score_scale)
    row_top = jnp.max(scores, axis=-1, keepdims=True)
    weights = jnp.exp(scores - row_top)
    row_total = jnp.sum(weights, axis=-1, keepdims=True)
    probs_low = (weights / row_total).astype(jnp.bfloat16)
    attended = jnp.einsum(
        "cgqk,kcd->qcgd", probs_low, value_rows, preferred_element_type=jnp.float32
    )
    return (attended, row_top + jnp.log(row_total))


def backward_block(queries, key_rows, value_rows, allow, log_total, grad_rows, score_scale):
    scores = block_scores(queries, key_rows, allow, score_scale)
    probs = jnp.exp(scores - log_total)
    grad_probs = jnp.einsum(
        "qcgd,kcd->cgqk", grad_rows, value_rows, preferred_element_type=jnp.float32
    )
    inner = jnp.sum(probs * grad_probs, axis=-1, keepdims=True)
    grad_scores = (probs * (grad_probs - inner)).astype(jnp.bfloat16)
    grad_queries = (
        jnp.einsum("cgqk,kcd->qcgd", grad_scores, key_rows, preferred_element_type=jnp.float32)
        * score_scale
    )
    grad_keys = (
        jnp.einsum("cgqk,qcgd->kcd", grad_scores, queries, preferred_element_type=jnp.float32)
        * score_scale
    )
    grad_values = jnp.einsum(
        "cgqk,qcgd->kcd", probs.astype(jnp.bfloat16), grad_rows, preferred_element_type=jnp.float32
    )
    return (grad_queries, grad_keys, grad_values)


def local(
    hidden_in,
    segments,
    routes,
    attn_gain,
    w_query,
    w_key,
    w_value,
    w_out,
    moe_gain,
    w_router,
    w_gate,
    w_up,
    w_down,
    d_out,
):
    tok_count, model_width = hidden_in.shape
    devices = lax.axis_size("dp")
    my_index = lax.axis_index("dp")
    num_experts = w_router.shape[1]
    split_ways = devices // num_experts
    groups = HEADS // KV_HEADS
    score_scale = 1.0 / math.sqrt(HEAD_DIM)
    places = jnp.arange(tok_count, dtype=jnp.int32)
    cosine, sine = rope_tables(my_index % 2 * tok_count + places, HEAD_DIM)
    seg_own = lax.dynamic_slice_in_dim(segments, my_index * tok_count, tok_count)
    seg_prev = lax.dynamic_slice_in_dim(
        segments, jnp.maximum(my_index - 1, 0) * tok_count, tok_count
    )
    prev_live = my_index % 2 == 1
    allow_prev = (seg_own[:, None] == seg_prev[None, :]) & prev_live
    allow_own = (seg_own[:, None] == seg_own[None, :]) & (places[None, :] <= places[:, None])
    allowed = jnp.concatenate([allow_prev, allow_own], axis=1)
    half_devices = devices // 2
    half_experts = num_experts // 2
    half = my_index // half_devices
    half_groups = [list(range(half_devices)), list(range(half_devices, devices))]
    across = [(i, (i + half_devices) % devices) for i in range(devices)]
    my_expert = my_index // split_ways
    far_routes, far_cot = lax.ppermute((routes, d_out), "dp", across)
    near_mask = member_mask(routes, num_experts)
    near_place = placement(near_mask, half * half_experts, half_experts)
    far_place = placement(
        member_mask(far_routes, num_experts), half * half_experts, half_experts
    )
    near_cot_rows = spread(near_place, d_out, half_experts, split_ways, half_groups)
    far_cot_rows = spread(far_place, far_cot, half_experts, split_ways, half_groups)
    x_float = hidden_in.astype(jnp.float32)
    h_one = rms_scale(x_float, attn_gain).astype(jnp.bfloat16)
    q_raw = jnp.dot(h_one, w_query, preferred_element_type=jnp.float32).reshape(
        tok_count, HEADS, HEAD_DIM
    )
    k_raw = jnp.dot(h_one, w_key, preferred_element_type=jnp.float32).reshape(
        tok_count, KV_HEADS, HEAD_DIM
    )
    v_low = (
        jnp.dot(h_one, w_value, preferred_element_type=jnp.float32)
        .astype(jnp.bfloat16)
        .reshape(tok_count, KV_HEADS, HEAD_DIM)
    )
    q_rot = rotate(q_raw, cosine, sine).astype(jnp.bfloat16)
    k_rot = rotate(k_raw, cosine, sine).astype(jnp.bfloat16)
    prev_keys, prev_values = passed_along((k_rot, v_low), "dp", 1)
    key_rows = jnp.concatenate([prev_keys, k_rot], axis=0)
    value_rows = jnp.concatenate([prev_values, v_low], axis=0)
    q_blocks = q_rot.reshape(tok_count, KV_HEADS, groups, HEAD_DIM)

    attended, log_total = forward_block(q_blocks, key_rows, value_rows, allowed, score_scale)
    o_low = attended.reshape(tok_count, HEADS * HEAD_DIM).astype(jnp.bfloat16)
    r_one = x_float + jnp.dot(o_low, w_out, preferred_element_type=jnp.float32)
    h_two = rms_scale(r_one, moe_gain).astype(jnp.bfloat16)
    logits = jnp.dot(h_two, w_router, preferred_element_type=jnp.float32)
    gates = jax.nn.softmax(jnp.where(near_mask, logits, -jnp.inf), axis=-1)
    gate_high, gate_rest = split_two(gates)
    pad = jnp.zeros((tok_count, 128 - 2 * num_experts), jnp.bfloat16)
    near_tokens = jnp.concatenate([h_two, gate_high, gate_rest, pad], axis=1)
    far_tokens = lax.ppermute(near_tokens, "dp", across)
    near_rows = spread(near_place, near_tokens, half_experts, split_ways, half_groups)
    far_rows = spread(far_place, far_tokens, half_experts, split_ways, half_groups)
    lane = jnp.arange(128, dtype=jnp.int32)
    lane_high = (lane == my_expert)[None, :]
    lane_rest = (lane == my_expert + num_experts)[None, :]

    def work(rows, cot_rows):
        tail = rows[:, model_width:].astype(jnp.float32)
        gate = jnp.sum(jnp.where(lane_high | lane_rest, tail, 0.0), axis=1, keepdims=True)
        rows = rows[:, :model_width]
        results = expert_block(rows, gate, cot_rows, w_gate, w_up, w_down)
        high, rest = split_two(results[5])
        extra = jnp.where(lane_high, high, jnp.where(lane_rest, rest, jnp.bfloat16(0)))
        return (rows,) + results[:4] + (jnp.concatenate([results[4], extra], axis=1), results[6])

    near = work(near_rows, near_cot_rows)
    far = work(far_rows, far_cot_rows)

    def combine(back, chosen):
        return dot_left_t(chosen, back)

    far_back, far_wide = bring_back(far_place, far[5], half_experts, split_ways, half_groups)
    near_back, near_wide = bring_back(near_place, near[5], half_experts, split_ways, half_groups)
    far_sum = lax.ppermute(combine(far_back, far_wide).astype(jnp.bfloat16), "dp", across)
    grad_tokens = combine(near_back, near_wide) + far_sum.astype(jnp.float32)
    near_out, far_out, _ = lax.optimization_barrier((near[6], far[6], near_back))
    far_ret, _ = bring_back(far_place, far_out, half_experts, split_ways, half_groups)
    near_ret, _ = bring_back(near_place, near_out, half_experts, split_ways, half_groups)
    far_mix = lax.ppermute(combine(far_ret, far_wide).astype(jnp.bfloat16), "dp", across)
    mixed = combine(near_ret, near_wide) + far_mix.astype(jnp.float32)
    out_hidden = (r_one + mixed).astype(jnp.bfloat16)
    grad_down = dot_left_t(near[1], near[2]) + dot_left_t(far[1], far[2])
    grad_gate = dot_left_t(near[0], near[3]) + dot_left_t(far[0], far[3])
    grad_up = dot_left_t(near[0], near[4]) + dot_left_t(far[0], far[4])
    cot_float = d_out.astype(jnp.float32)
    grad_h_two = grad_tokens[:, :model_width]
    grad_gates = (
        grad_tokens[:, model_width : model_width + num_experts]
        + grad_tokens[:, model_width + num_experts : model_width + 2 * num_experts]
    )
    gated_sum = jnp.sum(gates * grad_gates, axis=1, keepdims=True)
    grad_logits = (gates * (grad_gates - gated_sum)).astype(jnp.bfloat16)
    grad_router = dot_left_t(h_two, grad_logits)
    grad_h_two = grad_h_two + dot_right_t(grad_logits, w_router)
    _, norm_back_two = jax.vjp(rms_scale, r_one, moe_gain)
    grad_r_norm, grad_moe_gain = norm_back_two(grad_h_two)
    grad_r_one = cot_float + grad_r_norm
    grad_y_low = grad_r_one.astype(jnp.bfloat16)
    grad_out_t = dot_left_t(grad_y_low, o_low)
    out_part, out_extra = reduced(
        grad_out_t, jnp.concatenate([grad_router, grad_moe_gain[:, None]], axis=1), devices
    )
    grad_o_low = dot_right_t(grad_y_low, w_out).astype(jnp.bfloat16)
    grad_o_blocks = grad_o_low.reshape(tok_count, KV_HEADS, groups, HEAD_DIM)
    grad_q_blocks, grad_key_rows, grad_value_rows = backward_block(
        q_blocks, key_rows, value_rows, allowed, log_total, grad_o_blocks, score_scale
    )
    back_keys, back_values = (
        passed_along(grad_key_rows[:tok_count].astype(jnp.bfloat16), "dp", -1).astype(jnp.float32),
        passed_along(grad_value_rows[:tok_count].astype(jnp.bfloat16), "dp", -1).astype(
            jnp.float32
        ),
    )
    grad_k_rot = grad_key_rows[tok_count:] + back_keys
    grad_v_rows = grad_value_rows[tok_count:] + back_values
    grad_q_rot = grad_q_blocks.reshape(tok_count, HEADS, HEAD_DIM)
    grad_q_low = (
        unrotate(grad_q_rot, cosine, sine).reshape(tok_count, HEADS * HEAD_DIM).astype(jnp.bfloat16)
    )
    grad_k_low = (
        unrotate(grad_k_rot, cosine, sine)
        .reshape(tok_count, KV_HEADS * HEAD_DIM)
        .astype(jnp.bfloat16)
    )
    grad_v_low = grad_v_rows.reshape(tok_count, KV_HEADS * HEAD_DIM).astype(jnp.bfloat16)
    grad_query = dot_left_t(h_one, grad_q_low)
    grad_key = dot_left_t(h_one, grad_k_low)
    grad_value = dot_left_t(h_one, grad_v_low)
    grad_h_one = (
        dot_right_t(grad_q_low, w_query)
        + dot_right_t(grad_k_low, w_key)
        + dot_right_t(grad_v_low, w_value)
    )
    _, norm_back_one = jax.vjp(rms_scale, x_float, attn_gain)
    grad_x_norm, grad_attn_gain = norm_back_one(grad_h_one)
    grad_input = grad_r_one + grad_x_norm
    shared = jnp.concatenate([grad_query, grad_key, grad_value], axis=1)
    shared_part, shared_extra = reduced(shared, grad_attn_gain[:, None], devices)
    query_width, key_width = grad_query.shape[1], grad_key.shape[1]
    grad_query = shared_part[:, :query_width]
    grad_key = shared_part[:, query_width : query_width + key_width]
    grad_value = shared_part[:, query_width + key_width :]
    grad_attn_gain = shared_extra[:, 0]
    grad_out = out_part.T
    grad_router = out_extra[:, :num_experts]
    grad_moe_gain = out_extra[:, num_experts]
    return (
        out_hidden,
        grad_input,
        grad_attn_gain,
        grad_query,
        grad_key,
        grad_value,
        grad_out,
        grad_moe_gain,
        grad_router,
        grad_gate,
        grad_up,
        grad_down,
    )


def solution(mesh):
    return jax.shard_map(
        local,
        mesh=mesh,
        in_specs=(
            P("dp", None),
            P(),
            P("dp", None),
            P(),
            P(),
            P(),
            P(),
            P(),
            P(),
            P(),
            P(None, "dp"),
            P(None, "dp"),
            P("dp", None),
            P("dp", None),
        ),
        out_specs=(
            P("dp", None),
            P("dp", None),
            P("dp"),
            P("dp", None),
            P("dp", None),
            P("dp", None),
            P(None, "dp"),
            P("dp"),
            P("dp", None),
            P(None, "dp"),
            P(None, "dp"),
            P("dp", None),
        ),
        check_vma=False,
    )
```

```python
import math

import jax
import jax.numpy as jnp
from jax import lax
from jax.experimental import pallas as pl
from jax.experimental.pallas import tpu as pltpu
from jax.sharding import PartitionSpec as P

HEADS = 16
KV_HEADS = 8
HEAD_DIM = 64
TOP = 8
CAP = 80


EPSILON = 1e-06


def passed_along(value, axis, steps):
    count = lax.axis_size(axis)
    leading, last = (max(0, -steps), min(count, count - steps))
    return lax.ppermute(value, axis, [(source, source + steps) for source in range(leading, last)])


def rms_scale(values, gain):
    return values * lax.rsqrt(jnp.mean(values * values, axis=-1, keepdims=True) + EPSILON) * gain


def rope_tables(positions, head_size):
    half_size = head_size // 2
    freqs = jnp.power(10000.0, -jnp.arange(half_size, dtype=jnp.float32) / half_size)
    angles = positions.astype(jnp.float32)[:, None] * freqs[None, :]
    angles = jnp.concatenate([angles, angles], axis=1)
    return (jnp.cos(angles), jnp.sin(angles))


def rotate(values, cosine, sine):
    half_size = values.shape[-1] // 2
    turned = jnp.concatenate([-values[..., half_size:], values[..., :half_size]], axis=-1)
    return values * cosine[:, None, :] + turned * sine[:, None, :]


def unrotate(grads, cosine, sine):
    half_size = grads.shape[-1] // 2
    moved = grads * sine[:, None, :]
    return grads * cosine[:, None, :] + jnp.concatenate(
        [moved[..., half_size:], -moved[..., :half_size]], axis=-1
    )


def dot_right_t(left, right):
    return lax.dot_general(
        left, right, (((1,), (1,)), ((), ())), preferred_element_type=jnp.float32
    )


def dot_left_t(left, right):
    return lax.dot_general(
        left, right, (((0,), (0,)), ((), ())), preferred_element_type=jnp.float32
    )


def split_two(values):
    high = values.astype(jnp.bfloat16)
    rest = (values - high.astype(jnp.float32)).astype(jnp.bfloat16)
    return high, rest


def member_mask(route_rows, num_experts):
    ids = jnp.arange(num_experts, dtype=jnp.int32)
    return jnp.any(route_rows[:, :, None] == ids[None, None, :], axis=1)


def placement(mask, first, amount):
    tok_count = mask.shape[0]
    part = lax.dynamic_slice_in_dim(mask.astype(jnp.bfloat16), first, amount, axis=1)
    places = jnp.arange(tok_count, dtype=jnp.int32)
    earlier = (places[:, None] < places[None, :]).astype(jnp.bfloat16)
    ranks = dot_left_t(part, earlier)
    ranks = jnp.where(part.T > 0, ranks, -1.0)
    want = jnp.arange(CAP, dtype=jnp.int32).astype(jnp.float32)
    chosen = (ranks[:, None, :] == want[None, :, None]).astype(jnp.bfloat16)
    return chosen.reshape(amount * CAP, tok_count)


def spread(chosen, values, amount, split_ways, groups):
    width = values.shape[1]
    picked = jnp.dot(chosen, values, preferred_element_type=jnp.float32).astype(jnp.bfloat16)
    sent = jnp.broadcast_to(
        picked.reshape(amount, 1, CAP, width), (amount, split_ways, CAP, width)
    ).reshape(amount * split_ways, CAP, width)
    return lax.all_to_all(
        sent, "dp", split_axis=0, concat_axis=0, tiled=True, axis_index_groups=groups
    ).reshape(-1, width)


def bring_back(chosen, rows, amount, split_ways, groups):
    width = rows.shape[1]
    back = lax.all_to_all(
        rows.reshape(amount * split_ways, CAP, width),
        "dp",
        split_axis=0,
        concat_axis=0,
        tiled=True,
        axis_index_groups=groups,
    ).reshape(-1, width)
    if split_ways > 1:
        tok_count = chosen.shape[1]
        chosen = jnp.broadcast_to(
            chosen.reshape(amount, 1, CAP, tok_count), (amount, split_ways, CAP, tok_count)
        ).reshape(-1, tok_count)
    return back, chosen


def expert_kernel(
    rows_ref, cot_ref, sel_ref, gate_w_ref, up_w_ref, down_w_ref,
    back_ref, out_ref, hidden_ref, cot_out_ref, grad_gate_ref, grad_up_ref,
):
    width = cot_ref.shape[1]
    rows = rows_ref[:, :width]
    tail = rows_ref[:, width:].astype(jnp.float32)
    first, second = sel_ref[0:1, :], sel_ref[1:2, :]
    gate = jnp.sum(tail * (first + second), axis=1, keepdims=True)
    gate_pre = jnp.dot(rows, gate_w_ref[...], preferred_element_type=jnp.float32)
    up_pre = jnp.dot(rows, up_w_ref[...], preferred_element_type=jnp.float32)
    sigmoid = 1.0 / (1.0 + jnp.exp(-gate_pre))
    activated = gate_pre * sigmoid
    hidden = (activated * up_pre).astype(jnp.bfloat16)
    hidden_ref[...] = hidden
    cot_float = cot_ref[...].astype(jnp.float32)
    grad_rows = (gate * cot_float).astype(jnp.bfloat16)
    cot_out_ref[...] = grad_rows
    grad_hidden = dot_right_t(grad_rows, down_w_ref[...])
    grad_gate_pre = (grad_hidden * up_pre * (sigmoid * (1.0 + gate_pre * (1.0 - sigmoid)))).astype(
        jnp.bfloat16
    )
    grad_up_pre = (grad_hidden * activated).astype(jnp.bfloat16)
    grad_gate_ref[...] = grad_gate_pre
    grad_up_ref[...] = grad_up_pre
    back = dot_right_t(grad_gate_pre, gate_w_ref[...]) + dot_right_t(grad_up_pre, up_w_ref[...])
    expert_out = jnp.dot(hidden, down_w_ref[...], preferred_element_type=jnp.float32)
    grad_gates = jnp.sum(expert_out * cot_float, axis=1, keepdims=True)
    out_ref[...] = (gate * expert_out).astype(jnp.bfloat16)
    high = grad_gates.astype(jnp.bfloat16).astype(jnp.float32)
    back_ref[:, :width] = back.astype(jnp.bfloat16)
    back_ref[:, width:] = (high * first + (grad_gates - high) * second).astype(jnp.bfloat16)


def expert_block(rows, cot_rows, select, w_gate, w_up, w_down):
    count, wide = rows.shape
    width, inner = w_gate.shape
    tile = 4 * CAP
    by_row = lambda w: pl.BlockSpec((tile, w), lambda i: (i, 0))
    whole = lambda x: pl.BlockSpec(x.shape, lambda i: (0, 0))
    shape = lambda w: jax.ShapeDtypeStruct((count, w), jnp.bfloat16)
    widths = (wide, width, inner, width, inner, inner)
    return pl.pallas_call(
        expert_kernel,
        grid=(count // tile,),
        in_specs=[
            by_row(wide), by_row(width), whole(select), whole(w_gate), whole(w_up), whole(w_down)
        ],
        out_specs=[by_row(w) for w in widths],
        out_shape=[shape(w) for w in widths],
        compiler_params=pltpu.CompilerParams(vmem_limit_bytes=40 * 1024 * 1024),
        cost_estimate=pl.CostEstimate(
            flops=14 * count * width * inner,
            bytes_accessed=2 * (count * (wide + width + sum(widths)) + 3 * width * inner),
            transcendentals=count * inner,
        ),
    )(rows, cot_rows, select, w_gate, w_up, w_down)


def halves(values, devices):
    count, width = values.shape
    core = lax.axis_index("dp") % 2
    cut = values.reshape(count, devices // 8, 4, 2, width // devices)
    cut = cut.transpose(3, 0, 2, 1, 4).reshape(2, count, width // 2)
    keep = lax.dynamic_index_in_dim(cut, core, 0, keepdims=False)
    give = lax.dynamic_index_in_dim(cut, 1 - core, 0, keepdims=False)
    return keep, give


def with_partner(keep, give, devices):
    other = lax.ppermute(give, "dp", [(i, i ^ 1) for i in range(devices)])
    return jnp.concatenate([keep, other], axis=0)


def reduced(left_both, right, devices):
    right_both = with_partner(right, right, devices)
    total = dot_left_t(left_both, right_both)
    width = total.shape[1]
    rows = 2 * total.shape[0] // devices
    stage_groups = (
        [[8 * z + 2 * i + c for i in range(4)] for z in range(devices // 8) for c in range(2)],
        [[8 * z + i for z in range(devices // 8)] for i in range(8)],
    )
    total = total.reshape(4, devices // 8, rows, width)
    for groups in stage_groups:
        got = lax.all_to_all(
            total.astype(jnp.bfloat16),
            "dp",
            split_axis=0,
            concat_axis=0,
            tiled=True,
            axis_index_groups=groups,
        )
        total = jnp.sum(got.astype(jnp.float32), axis=0)
    return total


def block_scores(queries, key_rows, allow, score_scale):
    raw = jnp.einsum("qcgd,kcd->cgqk", queries, key_rows, preferred_element_type=jnp.float32)
    return jnp.where(allow[None, None], raw * score_scale, -1e30)


def forward_block(queries, key_rows, value_rows, allow, score_scale):
    scores = block_scores(queries, key_rows, allow, score_scale)
    row_top = jnp.max(scores, axis=-1, keepdims=True)
    weights = jnp.exp(scores - row_top)
    row_total = jnp.sum(weights, axis=-1, keepdims=True)
    probs_low = (weights / row_total).astype(jnp.bfloat16)
    attended = jnp.einsum(
        "cgqk,kcd->qcgd", probs_low, value_rows, preferred_element_type=jnp.float32
    )
    return (attended, row_top + jnp.log(row_total))


def backward_block(queries, key_rows, value_rows, allow, log_total, grad_rows, score_scale):
    scores = block_scores(queries, key_rows, allow, score_scale)
    probs = jnp.exp(scores - log_total)
    grad_probs = jnp.einsum(
        "qcgd,kcd->cgqk", grad_rows, value_rows, preferred_element_type=jnp.float32
    )
    inner = jnp.sum(probs * grad_probs, axis=-1, keepdims=True)
    grad_scores = (probs * (grad_probs - inner)).astype(jnp.bfloat16)
    grad_queries = (
        jnp.einsum("cgqk,kcd->qcgd", grad_scores, key_rows, preferred_element_type=jnp.float32)
        * score_scale
    )
    grad_keys = (
        jnp.einsum("cgqk,qcgd->kcd", grad_scores, queries, preferred_element_type=jnp.float32)
        * score_scale
    )
    grad_values = jnp.einsum(
        "cgqk,qcgd->kcd", probs.astype(jnp.bfloat16), grad_rows, preferred_element_type=jnp.float32
    )
    return (grad_queries, grad_keys, grad_values)


def local(
    hidden_in,
    segments,
    routes,
    attn_gain,
    w_query,
    w_key,
    w_value,
    w_out,
    moe_gain,
    w_router,
    w_gate,
    w_up,
    w_down,
    d_out,
):
    tok_count, model_width = hidden_in.shape
    devices = lax.axis_size("dp")
    my_index = lax.axis_index("dp")
    num_experts = w_router.shape[1]
    split_ways = devices // num_experts
    groups = HEADS // KV_HEADS
    score_scale = 1.0 / math.sqrt(HEAD_DIM)
    places = jnp.arange(tok_count, dtype=jnp.int32)
    cosine, sine = rope_tables(my_index % 2 * tok_count + places, HEAD_DIM)
    seg_own = lax.dynamic_slice_in_dim(segments, my_index * tok_count, tok_count)
    seg_prev = lax.dynamic_slice_in_dim(
        segments, jnp.maximum(my_index - 1, 0) * tok_count, tok_count
    )
    prev_live = my_index % 2 == 1
    allow_prev = (seg_own[:, None] == seg_prev[None, :]) & prev_live
    allow_own = (seg_own[:, None] == seg_own[None, :]) & (places[None, :] <= places[:, None])
    allowed = jnp.concatenate([allow_prev, allow_own], axis=1)
    half_devices = devices // 2
    half_experts = num_experts // 2
    half = my_index // half_devices
    half_groups = [list(range(half_devices)), list(range(half_devices, devices))]
    across = [(i, (i + half_devices) % devices) for i in range(devices)]
    my_expert = my_index // split_ways
    far_routes, far_cot = lax.ppermute((routes, d_out), "dp", across)
    near_mask = member_mask(routes, num_experts)
    near_place = placement(near_mask, half * half_experts, half_experts)
    far_place = placement(
        member_mask(far_routes, num_experts), half * half_experts, half_experts
    )
    near_cot_rows = spread(near_place, d_out, half_experts, split_ways, half_groups)
    x_float = hidden_in.astype(jnp.float32)
    h_one = rms_scale(x_float, attn_gain).astype(jnp.bfloat16)
    h_one_both = with_partner(*halves(h_one, devices), devices)
    q_raw = jnp.dot(h_one, w_query, preferred_element_type=jnp.float32).reshape(
        tok_count, HEADS, HEAD_DIM
    )
    k_raw = jnp.dot(h_one, w_key, preferred_element_type=jnp.float32).reshape(
        tok_count, KV_HEADS, HEAD_DIM
    )
    v_low = (
        jnp.dot(h_one, w_value, preferred_element_type=jnp.float32)
        .astype(jnp.bfloat16)
        .reshape(tok_count, KV_HEADS, HEAD_DIM)
    )
    q_rot = rotate(q_raw, cosine, sine).astype(jnp.bfloat16)
    k_rot = rotate(k_raw, cosine, sine).astype(jnp.bfloat16)
    prev_keys, prev_values = passed_along((k_rot, v_low), "dp", 1)
    key_rows = jnp.concatenate([prev_keys, k_rot], axis=0)
    value_rows = jnp.concatenate([prev_values, v_low], axis=0)
    q_blocks = q_rot.reshape(tok_count, KV_HEADS, groups, HEAD_DIM)

    attended, log_total = forward_block(q_blocks, key_rows, value_rows, allowed, score_scale)
    attended, far_cot = lax.optimization_barrier((attended, far_cot))
    far_cot_rows = spread(far_place, far_cot, half_experts, split_ways, half_groups)
    o_low = attended.reshape(tok_count, HEADS * HEAD_DIM).astype(jnp.bfloat16)
    r_one = x_float + jnp.dot(o_low, w_out, preferred_element_type=jnp.float32)
    h_two = rms_scale(r_one, moe_gain).astype(jnp.bfloat16)
    logits = jnp.dot(h_two, w_router, preferred_element_type=jnp.float32)
    gates = jax.nn.softmax(jnp.where(near_mask, logits, -jnp.inf), axis=-1)
    gate_high, gate_rest = split_two(gates)
    pad = jnp.zeros((tok_count, 128 - 2 * num_experts), jnp.bfloat16)
    near_tokens = jnp.concatenate([h_two, gate_high, gate_rest, pad], axis=1)
    far_tokens = lax.ppermute(near_tokens, "dp", across)
    near_rows = spread(near_place, near_tokens, half_experts, split_ways, half_groups)
    far_rows = spread(far_place, far_tokens, half_experts, split_ways, half_groups)
    lane = jnp.arange(128, dtype=jnp.int32)
    lane_high = (lane == my_expert)[None, :]
    lane_rest = (lane == my_expert + num_experts)[None, :]

    select = jnp.concatenate(
        [lane_high, lane_rest, jnp.zeros((6, 128), jnp.bool_)], axis=0
    ).astype(jnp.float32)
    near = expert_block(near_rows, near_cot_rows, select, w_gate, w_up, w_down)
    near_sent, far_rows = lax.optimization_barrier((near[0], far_rows))
    far = expert_block(far_rows, far_cot_rows, select, w_gate, w_up, w_down)

    def combine(back, chosen):
        return dot_left_t(chosen, back)

    near_back, near_wide = bring_back(near_place, near_sent, half_experts, split_ways, half_groups)
    far_back, far_wide = bring_back(far_place, far[0], half_experts, split_ways, half_groups)
    far_sum = lax.ppermute(combine(far_back, far_wide).astype(jnp.bfloat16), "dp", across)
    grad_tokens = combine(near_back, near_wide) + far_sum.astype(jnp.float32)
    near_out, far_out, _ = lax.optimization_barrier((near[1], far[1], far_back))
    far_ret, _ = bring_back(far_place, far_out, half_experts, split_ways, half_groups)
    near_ret, _ = bring_back(near_place, near_out, half_experts, split_ways, half_groups)
    far_mix = lax.ppermute(combine(far_ret, far_wide).astype(jnp.bfloat16), "dp", across)
    mixed = combine(near_ret, near_wide) + far_mix.astype(jnp.float32)
    out_hidden = (r_one + mixed).astype(jnp.bfloat16)
    grad_down = dot_left_t(near[2], near[3]) + dot_left_t(far[2], far[3])
    near_lone, far_lone = near_rows[:, :model_width], far_rows[:, :model_width]
    grad_gate = dot_left_t(near_lone, near[4]) + dot_left_t(far_lone, far[4])
    grad_up = dot_left_t(near_lone, near[5]) + dot_left_t(far_lone, far[5])
    cot_float = d_out.astype(jnp.float32)
    grad_h_two = grad_tokens[:, :model_width]
    grad_gates = (
        grad_tokens[:, model_width : model_width + num_experts]
        + grad_tokens[:, model_width + num_experts : model_width + 2 * num_experts]
    )
    gated_sum = jnp.sum(gates * grad_gates, axis=1, keepdims=True)
    grad_logits = (gates * (grad_gates - gated_sum)).astype(jnp.bfloat16)
    grad_router = dot_left_t(h_two, grad_logits)
    grad_h_two = grad_h_two + dot_right_t(grad_logits, w_router)
    _, norm_back_two = jax.vjp(rms_scale, r_one, moe_gain)
    grad_r_norm, grad_moe_gain = norm_back_two(grad_h_two)
    grad_r_one = cot_float + grad_r_norm
    grad_y_low = grad_r_one.astype(jnp.bfloat16)
    grad_y_both = with_partner(*halves(grad_y_low, devices), devices)
    out_part = reduced(grad_y_both, o_low, devices)
    grad_o_low = dot_right_t(grad_y_low, w_out).astype(jnp.bfloat16)
    grad_o_blocks = grad_o_low.reshape(tok_count, KV_HEADS, groups, HEAD_DIM)
    grad_q_blocks, grad_key_rows, grad_value_rows = backward_block(
        q_blocks, key_rows, value_rows, allowed, log_total, grad_o_blocks, score_scale
    )
    back_keys, back_values = (
        passed_along(grad_key_rows[:tok_count].astype(jnp.bfloat16), "dp", -1).astype(jnp.float32),
        passed_along(grad_value_rows[:tok_count].astype(jnp.bfloat16), "dp", -1).astype(
            jnp.float32
        ),
    )
    grad_k_rot = grad_key_rows[tok_count:] + back_keys
    grad_v_rows = grad_value_rows[tok_count:] + back_values
    grad_q_rot = grad_q_blocks.reshape(tok_count, HEADS, HEAD_DIM)
    grad_q_low = (
        unrotate(grad_q_rot, cosine, sine).reshape(tok_count, HEADS * HEAD_DIM).astype(jnp.bfloat16)
    )
    grad_k_low = (
        unrotate(grad_k_rot, cosine, sine)
        .reshape(tok_count, KV_HEADS * HEAD_DIM)
        .astype(jnp.bfloat16)
    )
    grad_v_low = grad_v_rows.reshape(tok_count, KV_HEADS * HEAD_DIM).astype(jnp.bfloat16)
    shared = jnp.concatenate([grad_q_low, grad_k_low, grad_v_low], axis=1)
    shared_part = reduced(h_one_both, shared, devices)
    grad_h_one = (
        dot_right_t(grad_q_low, w_query)
        + dot_right_t(grad_k_low, w_key)
        + dot_right_t(grad_v_low, w_value)
    )
    _, norm_back_one = jax.vjp(rms_scale, x_float, attn_gain)
    grad_x_norm, grad_attn_gain = norm_back_one(grad_h_one)
    grad_input = grad_r_one + grad_x_norm
    few = jnp.concatenate(
        [grad_router, grad_moe_gain[:, None], grad_attn_gain[:, None]], axis=1
    ).reshape(devices, -1)
    few = lax.all_to_all(few, "dp", split_axis=0, concat_axis=0, tiled=True)
    few = jnp.sum(few, axis=0).reshape(-1, num_experts + 2)
    query_width, key_width = w_query.shape[1], w_key.shape[1]
    grad_query = shared_part[:, :query_width]
    grad_key = shared_part[:, query_width : query_width + key_width]
    grad_value = shared_part[:, query_width + key_width :]
    grad_attn_gain = few[:, num_experts + 1]
    grad_out = out_part.T
    grad_router = few[:, :num_experts]
    grad_moe_gain = few[:, num_experts]
    return (
        out_hidden,
        grad_input,
        grad_attn_gain,
        grad_query,
        grad_key,
        grad_value,
        grad_out,
        grad_moe_gain,
        grad_router,
        grad_gate,
        grad_up,
        grad_down,
    )


def solution(mesh):
    return jax.shard_map(
        local,
        mesh=mesh,
        in_specs=(
            P("dp", None),
            P(),
            P("dp", None),
            P(),
            P(),
            P(),
            P(),
            P(),
            P(),
            P(),
            P(None, "dp"),
            P(None, "dp"),
            P("dp", None),
            P("dp", None),
        ),
        out_specs=(
            P("dp", None),
            P("dp", None),
            P("dp"),
            P("dp", None),
            P("dp", None),
            P("dp", None),
            P(None, "dp"),
            P("dp"),
            P("dp", None),
            P(None, "dp"),
            P(None, "dp"),
            P("dp", None),
        ),
        check_vma=False,
    )
```
